128 devices in a mesh: vc: 8 (over x, core), vd: 16 (over z, y).
Axes of the slice: x: 4, y: 4, z: 4, core: 2. Of those that a mesh axis runs over, the one named last changes fastest.
Arguments:
- integrals: bfloat16 [2048, 262144], P(('vc', 'vd')), may hold values from -0.015625 to 0.015625
- amplitudes: bfloat16 [2048, 262144], P(('vc', 'vd')), may hold values from -6 to 6
- block_lists: int32 [128, 15], replicated, may hold values from -1 to 2047, as said below
Outputs:
- ladder: float32 [2048, 2048], P(('vc', 'vd'))
The draws below stay inside these ranges and needn't reach their ends.
Inputs may be any that keep to these rules, and one draw needn't show every extreme that they name: `block_lists`: row r lists in its first slots the screened blocks of device r (index along vc+vd), then -1 in the rest; no block appears twice in the whole array; each row holds 1 to 15 blocks and some row exactly 15; exactly 1024 entries are blocks.
All inputs are finite; a program needn't handle non-finite values.
Results may differ from the reference program's by a relative error of at most 0.0003.
Values may be sent and summed in bfloat16 or wider, within the bound.
A program may use at most 128 MiB of HBM per device.

```python
import jax
import jax.numpy as jnp
from jax import lax

BW = 128
LIVE_DEV = 8
MOSTB = 15
LIVE = 1024
NB = 2048
CD = 262144
AROWS = 2048
PAIRS = 2048


def draw_block_lists(key, part):
    key = jax.random.fold_in(key, 11)
    key_count, key_order, key_blocks = jax.random.split(key, 3)
    owner_count = NB // (2 * LIVE_DEV)
    half_count = owner_count // 2
    first = jax.random.randint(key_count, (half_count,), 1, 2 * LIVE_DEV, dtype=jnp.int32)
    first = first.at[0].set(MOSTB)
    counts = jnp.concatenate([first, 2 * LIVE_DEV - first]).astype(jnp.int32)
    counts = jax.random.permutation(key_order, counts)
    offsets = jnp.cumsum(counts) - counts
    shuffled = jax.random.permutation(key_blocks, NB).astype(jnp.int32)
    slot_ids = jnp.arange(MOSTB, dtype=jnp.int32)
    where_ids = jnp.clip(offsets[:, None] + slot_ids[None, :], 0, NB - 1)
    is_used = slot_ids[None, :] < counts[:, None]
    return jnp.where(is_used, shuffled[where_ids], -1).astype(jnp.int32)


def block_scale(key, dims, shards, least, top_value):
    def one(axis_at, blocks):
        steps = jax.random.uniform(jax.random.fold_in(jax.random.fold_in(key, 6), axis_at), (blocks,), jnp.float32, least / len(shards), top_value / len(shards))
        return jnp.repeat(jnp.exp(steps), dims[axis_at] // blocks).reshape((-1,) + (1,) * (len(dims) - axis_at - 1))

    loudness = one(*shards[0])
    for cut in shards[1:]:
        loudness = loudness * one(*cut)
    return loudness


def noise(key, shape, spread, most, cuts=(), kind=jnp.bfloat16):
    array = jax.random.normal(key, shape, jnp.float32) * spread
    if len(cuts) > 0:
        array = block_scale(key, shape, cuts, -0.22, 0.18) * array
    return jnp.clip(array, min=-most, max=most).astype(kind)


def setup_inputs(seed: int = 0) -> dict:
    splits = jax.random.split(jax.random.key(seed), 4)
    integrals = noise(splits[0], (AROWS, CD), (LIVE * BW) ** -0.5, 0.015625, ((0, 128),))
    amplitudes = noise(splits[1], (PAIRS, CD), 1.0, 6.0, ((0, 128),))
    block_lists = draw_block_lists(jax.random.fold_in(splits[3], 71), 0)
    return {"integrals": integrals, "amplitudes": amplitudes, "block_lists": block_lists}


def reference(integrals, amplitudes, block_lists):
    flat_list = block_lists.reshape(-1)
    listed = jnp.sort(flat_list)[flat_list.shape[0] - LIVE:].astype(jnp.int32)
    group_size = 64
    groups = listed.reshape(LIVE // group_size, group_size)
    amp_blocks = amplitudes.reshape(PAIRS, NB, BW)
    int_blocks = integrals.reshape(AROWS, NB, BW)

    def add_group(total, ids):
        amp_part = jnp.take(amp_blocks, ids, axis=1).reshape(PAIRS, group_size * BW).astype(jnp.float32)
        int_part = jnp.take(int_blocks, ids, axis=1).reshape(AROWS, group_size * BW).astype(jnp.float32)
        term = lax.dot_general(amp_part, int_part, (((1,), (1,)), ((), ())), precision=lax.Precision.HIGHEST, preferred_element_type=jnp.float32)
        return total + term, None

    start = jnp.zeros((PAIRS, AROWS), jnp.float32)
    ladder, unused = lax.scan(add_group, start, groups)
    return ladder
```

```python
import functools
import random

import jax
import jax.numpy as jnp
from jax import lax
from jax.experimental import pallas as pl
from jax.experimental.pallas import tpu as pltpu
from jax.sharding import PartitionSpec as P

MESH = pl.DeviceIdType.MESH
BW = 128
NX, NC, NY, NZ = 4, 2, 4, 4
GROUP = NX * NC * NY
LISTED = 1024
MIB = 1 << 20


def plane_index(x, c, y):
    return (x * NC + c) * NY + y


def device(x, c, y, z):
    return (x * NC + c, z * NY + y)


def wait_bytes(ref, sem):
    pltpu.make_async_copy(ref, ref, sem).wait()


def list_blocks(lists, ids):
    slots = lists.shape[1]

    def one(row, filled):
        used = jnp.int32(0)
        for slot in range(slots):
            block = lists[row, slot]
            ids[filled + slot] = block
            used += (block >= 0).astype(jnp.int32)
        return filled + used

    lax.fori_loop(0, lists.shape[0], one, jnp.int32(0))


def kernel(
    steps, ahead, ids, amp_hbm, int_hbm, out_ref,
    amp, integ, packed, own, amp_z, int_z, total, half, part_x, part_y, sum_x, sum_y, end_y, end_x, done, other,
    load_sem, send_sem, recv_sem, zsend_sem, zrecv_sem, rsend_sem, rrecv_sem,
):
    vc, vd = lax.axis_index("vc"), lax.axis_index("vd")
    x, c, z, y = vc // NC, lax.rem(vc, NC), vd // NY, lax.rem(vd, NY)
    me = plane_index(x, c, y)
    amp_peer = device(x, c, y, 3 - z)
    int_peer = device(x, c, y, z + 1 - 2 * lax.rem(z, 2))
    order = [(dx, dc, dy) for dx in range(NX) for dc in range(NC) for dy in range(NY)][1:]
    random.Random(2).shuffle(order)
    peers = []
    for dx, dc, dy in order:
        px, pc, py = lax.rem(x + dx, NX), lax.rem(c + dc, NC), lax.rem(y + dy, NY)
        peers.append((plane_index(px, pc, py), device(px, pc, py, z)))
    columns = packed.shape[3]
    blocks = columns // BW

    loads = [
        pltpu.make_async_copy(amp_hbm, amp, load_sem.at[0]),
        pltpu.make_async_copy(int_hbm, integ, load_sem.at[1]),
    ]
    for load in loads:
        load.start()
    barrier = pltpu.get_barrier_semaphore()
    everyone = [place for _, place in peers] + [amp_peer, int_peer]
    for place in everyone:
        pl.semaphore_signal(barrier, inc=1, device_id=place, device_id_type=MESH)
    total[...] = jnp.zeros_like(total)
    for load in loads:
        load.wait()

    def pack(step):
        def one(member, carry):
            for block in range(blocks):
                start = ids[(step * GROUP + member) * blocks + block] * BW
                packed[step, member, 0:16, block * BW:(block + 1) * BW] = amp[:, pl.ds(start, BW)]
                packed[step, member, 16:32, block * BW:(block + 1) * BW] = integ[:, pl.ds(start, BW)]
            return carry

        lax.fori_loop(0, GROUP, one, 0)

    def send(step):
        for index, place in peers:
            pltpu.make_async_remote_copy(
                src_ref=packed.at[step, index], dst_ref=own.at[step, me],
                send_sem=send_sem, recv_sem=recv_sem.at[step], device_id=place, device_id_type=MESH,
            ).start()
        pltpu.make_async_copy(packed.at[step, me], own.at[step, me], recv_sem.at[step]).start()

    def pass_on(step):
        wait_bytes(own.at[step], recv_sem.at[step])
        pltpu.make_async_remote_copy(
            src_ref=own.at[step, :, 0:16, :], dst_ref=amp_z.at[step],
            send_sem=zsend_sem, recv_sem=zrecv_sem.at[0, step], device_id=amp_peer, device_id_type=MESH,
        ).start()
        pltpu.make_async_remote_copy(
            src_ref=own.at[step, :, 16:32, :], dst_ref=int_z.at[step],
            send_sem=zsend_sem, recv_sem=zrecv_sem.at[1, step], device_id=int_peer, device_id_type=MESH,
        ).start()

    def multiply(step):
        wait_bytes(amp_z.at[step], zrecv_sem.at[0, step])
        wait_bytes(int_z.at[step], zrecv_sem.at[1, step])
        rows = GROUP * 16
        lhs = [own[step, :, 0:16, :].reshape(rows, columns), amp_z[step].reshape(rows, columns)]
        for n in range(4):
            pieces = []
            for xc in (2 * n, 2 * n + 1):
                pieces.append(own[step, NY * xc:NY * (xc + 1), 16:32, :].reshape(64, columns))
                pieces.append(int_z[step, NY * xc:NY * (xc + 1)].reshape(64, columns))
            rhs = jnp.concatenate(pieces, axis=0)
            for which in range(2):
                term = lax.dot_general(lhs[which], rhs, (((1,), (1,)), ((), ())), preferred_element_type=jnp.float32)
                total[n, which] += term.reshape(NX, NC, NY, 16, 256)

    pack(0)
    pl.semaphore_wait(barrier, len(everyone))
    send(0)
    for step in range(1, ahead):
        pack(step)
        send(step)

    def turn(step, carry):
        pack(step + ahead)
        send(step + ahead)
        pass_on(step)

        @pl.when(step > 0)
        def _():
            multiply(step - 1)

        return carry

    lax.fori_loop(0, steps - ahead, turn, 0)

    def last(step, carry):
        pass_on(step)
        multiply(step - 1)
        return carry

    lax.fori_loop(steps - ahead, steps, last, 0)
    multiply(steps - 1)

    copy = pltpu.make_async_remote_copy(
        src_ref=total.at[:, :, :, 1 - c], dst_ref=half, send_sem=rsend_sem.at[0], recv_sem=rrecv_sem.at[0],
        device_id=device(x, 1 - c, y, z), device_id_type=MESH,
    )
    copy.start()
    copy.wait()
    half[...] += total[:, :, :, c]

    copies = []
    for d in (1, 2, 3):
        px, py = lax.rem(x + d, NX), lax.rem(y + d, NY)
        copies.append(pltpu.make_async_remote_copy(
            src_ref=half.at[0:2, :, px], dst_ref=part_x.at[d - 1], send_sem=rsend_sem.at[d], recv_sem=rrecv_sem.at[d],
            device_id=device(px, c, y, z), device_id_type=MESH,
        ))
        copies.append(pltpu.make_async_remote_copy(
            src_ref=half.at[2:4, :, :, py], dst_ref=part_y.at[d - 1], send_sem=rsend_sem.at[3 + d], recv_sem=rrecv_sem.at[3 + d],
            device_id=device(x, c, py, z), device_id_type=MESH,
        ))
    for copy in copies:
        copy.start()
    for copy in copies:
        copy.wait()
    sum_x[...] = half[0:2, :, x] + part_x[0] + part_x[1] + part_x[2]
    sum_y[...] = half[2:4, :, :, y] + part_y[0] + part_y[1] + part_y[2]

    copies = []
    for d in (1, 2, 3):
        px, py = lax.rem(x + d, NX), lax.rem(y + d, NY)
        copies.append(pltpu.make_async_remote_copy(
            src_ref=sum_x.at[:, :, py], dst_ref=end_y.at[d - 1], send_sem=rsend_sem.at[6 + d], recv_sem=rrecv_sem.at[6 + d],
            device_id=device(x, c, py, z), device_id_type=MESH,
        ))
        copies.append(pltpu.make_async_remote_copy(
            src_ref=sum_y.at[:, :, px], dst_ref=end_x.at[d - 1], send_sem=rsend_sem.at[9 + d], recv_sem=rrecv_sem.at[9 + d],
            device_id=device(px, c, y, z), device_id_type=MESH,
        ))
    for copy in copies:
        copy.start()
    for copy in copies:
        copy.wait()
    done[0:2] = sum_x[:, :, y] + end_y[0] + end_y[1] + end_y[2]
    done[2:4] = sum_y[:, :, x] + end_x[0] + end_x[1] + end_x[2]

    copy = pltpu.make_async_remote_copy(
        src_ref=done.at[:, 1], dst_ref=other, send_sem=rsend_sem.at[13], recv_sem=rrecv_sem.at[13],
        device_id=amp_peer, device_id_type=MESH,
    )
    copy.start()
    odd, high = lax.rem(z, 2), z // 2

    def place(values, n, swap, upper):
        for j in range(2):
            piece = values[:, j * BW:(j + 1) * BW]
            piece = jnp.where(swap == 1, pltpu.roll(piece, BW // 2, 1), piece)
            start = pl.multiple_of((2 * n + j) * 2 * BW + upper * BW, BW)
            out_ref[:, pl.ds(start, BW)] = piece

    for n in range(4):
        place(done[n, 0], n, odd, high)
    copy.wait()
    for n in range(4):
        place(other[n], n, 1 - odd, 1 - high)

    for _ in range(steps):
        wait_bytes(packed.at[0, 0:GROUP - 1], send_sem)
        wait_bytes(own.at[0], zsend_sem)


def solution(mesh):
    steps, ahead = 16, 2

    def shards(integrals, amplitudes, block_lists):
        columns = LISTED * BW // GROUP // steps
        f32, bf16 = jnp.float32, jnp.bfloat16
        ids = pl.pallas_call(
            list_blocks,
            out_shape=jax.ShapeDtypeStruct((LISTED + 16,), jnp.int32),
            in_specs=[pl.BlockSpec(memory_space=pltpu.SMEM)],
            out_specs=pl.BlockSpec(memory_space=pltpu.SMEM),
            name="list_blocks",
        )(block_lists)
        return pl.pallas_call(
            functools.partial(kernel, steps, ahead),
            out_shape=jax.ShapeDtypeStruct((16, 2048), f32),
            in_specs=[
                pl.BlockSpec(memory_space=pltpu.SMEM),
                pl.BlockSpec(memory_space=pl.ANY),
                pl.BlockSpec(memory_space=pl.ANY),
            ],
            out_specs=pl.BlockSpec(memory_space=pltpu.VMEM),
            scratch_shapes=[
                pltpu.VMEM(amplitudes.shape, bf16),
                pltpu.VMEM(integrals.shape, bf16),
                pltpu.VMEM((steps, GROUP, 32, columns), bf16),
                pltpu.VMEM((steps, GROUP, 32, columns), bf16),
                pltpu.VMEM((steps, GROUP, 16, columns), bf16),
                pltpu.VMEM((steps, GROUP, 16, columns), bf16),
                pltpu.VMEM((4, 2, NX, NC, NY, 16, 256), f32),
                pltpu.VMEM((4, 2, NX, NY, 16, 256), f32),
                pltpu.VMEM((3, 2, 2, NY, 16, 256), f32),
                pltpu.VMEM((3, 2, 2, NX, 16, 256), f32),
                pltpu.VMEM((2, 2, NY, 16, 256), f32),
                pltpu.VMEM((2, 2, NX, 16, 256), f32),
                pltpu.VMEM((3, 2, 2, 16, 256), f32),
                pltpu.VMEM((3, 2, 2, 16, 256), f32),
                pltpu.VMEM((4, 2, 16, 256), f32),
                pltpu.VMEM((4, 16, 256), f32),
                pltpu.SemaphoreType.DMA((2,)),
                pltpu.SemaphoreType.DMA,
                pltpu.SemaphoreType.DMA((steps,)),
                pltpu.SemaphoreType.DMA,
                pltpu.SemaphoreType.DMA((2, steps)),
                pltpu.SemaphoreType.DMA((14,)),
                pltpu.SemaphoreType.DMA((14,)),
            ],
            compiler_params=pltpu.CompilerParams(
                collective_id=0, has_side_effects=True, vmem_limit_bytes=62 * MIB
            ),
            name="ladder",
        )(ids, amplitudes, integrals)

    return jax.shard_map(
        shards,
        mesh=mesh,
        in_specs=(P(("vc", "vd"), None), P(("vc", "vd"), None), P()),
        out_specs=P(("vc", "vd"), None),
        check_vma=False,
    )
```

```python
import functools
import random

import jax
import jax.numpy as jnp
from jax import lax
from jax.experimental import pallas as pl
from jax.experimental.pallas import tpu as pltpu
from jax.sharding import PartitionSpec as P

MESH = pl.DeviceIdType.MESH
BW = 128
NX, NC, NY, NZ = 4, 2, 4, 4
GROUP = NX * NY
LISTED = 1024
MIB = 1 << 20


def device(x, c, y, z):
    return (x * NC + c, z * NY + y)


def wait_bytes(ref, sem):
    pltpu.make_async_copy(ref, ref, sem).wait()


def kernel(
    steps, ahead, lists, amp_hbm, int_hbm, out_ref,
    amp, integ, packed, own, amp_z, int_z, near, total, part_x, part_y, sum_x, sum_y, end_y, end_x, done, other,
    load_sem, send_sem, recv_sem, zsend_sem, zrecv_sem, nsend_sem, nrecv_sem, rsend_sem, rrecv_sem, last_sem,
):
    vc, vd = lax.axis_index("vc"), lax.axis_index("vd")
    x, c, z, y = vc // NC, lax.rem(vc, NC), vd // NY, lax.rem(vd, NY)
    me = x * NY + y
    amp_peer = device(x, c, y, 3 - z)
    int_peer = device(x, c, y, z + 1 - 2 * lax.rem(z, 2))
    near_peer = device(x, 1 - c, y, z)
    order = [(dx, dy) for dx in range(NX) for dy in range(NY)][1:]
    random.Random(1).shuffle(order)
    peers = []
    for dx, dy in order:
        px, py = lax.rem(x + dx, NX), lax.rem(y + dy, NY)
        peers.append((px * NY + py, device(px, c, py, z)))
    columns = packed.shape[3]
    blocks = columns // BW
    slots, owners = lists.shape

    loads = [
        pltpu.make_async_copy(amp_hbm, amp, load_sem.at[0]),
        pltpu.make_async_copy(int_hbm, integ, load_sem.at[1]),
    ]
    for load in loads:
        load.start()
    barrier = pltpu.get_barrier_semaphore()
    everyone = [place for _, place in peers] + [amp_peer, int_peer, near_peer]
    for place in everyone:
        pl.semaphore_signal(barrier, inc=1, device_id=place, device_id_type=MESH)
    total[...] = jnp.zeros_like(total)
    for load in loads:
        load.wait()

    def pack(step, state):
        def one(member, state):
            owner, slot = state
            for block in range(blocks):
                start = lists[slot, owner] * BW
                packed[step, member, 0:16, block * BW:(block + 1) * BW] = amp[:, pl.ds(start, BW)]
                packed[step, member, 16:32, block * BW:(block + 1) * BW] = integ[:, pl.ds(start, BW)]
                following = lists[jnp.minimum(slot + 1, slots - 1), owner]
                stays = jnp.logical_and(slot + 1 < slots, following >= 0)
                slot = jnp.where(stays, slot + 1, 0)
                owner = jnp.minimum(jnp.where(stays, owner, owner + 1), owners - 1)
            return owner, slot

        return lax.fori_loop(0, GROUP, one, state)

    def send(step):
        for index, place in peers:
            pltpu.make_async_remote_copy(
                src_ref=packed.at[step, index], dst_ref=own.at[step, me],
                send_sem=send_sem, recv_sem=recv_sem.at[step], device_id=place, device_id_type=MESH,
            ).start()
        pltpu.make_async_copy(packed.at[step, me], own.at[step, me], recv_sem.at[step]).start()

    def pass_on(step):
        wait_bytes(own.at[step], recv_sem.at[step])
        pltpu.make_async_remote_copy(
            src_ref=own.at[step, :, 16:32, :], dst_ref=int_z.at[step],
            send_sem=zsend_sem, recv_sem=zrecv_sem.at[1, step], device_id=int_peer, device_id_type=MESH,
        ).start()
        pltpu.make_async_remote_copy(
            src_ref=own.at[step, :, 0:16, :], dst_ref=amp_z.at[step],
            send_sem=zsend_sem, recv_sem=zrecv_sem.at[0, step], device_id=amp_peer, device_id_type=MESH,
        ).start()
        pltpu.make_async_remote_copy(
            src_ref=own.at[step, :, 16:32, :], dst_ref=near.at[step, 0],
            send_sem=nsend_sem, recv_sem=nrecv_sem.at[0, step], device_id=near_peer, device_id_type=MESH,
        ).start()

    def relay(step):
        wait_bytes(int_z.at[step], zrecv_sem.at[1, step])
        pltpu.make_async_remote_copy(
            src_ref=int_z.at[step], dst_ref=near.at[step, 1],
            send_sem=nsend_sem, recv_sem=nrecv_sem.at[1, step], device_id=near_peer, device_id_type=MESH,
        ).start()

    def arrive(step):
        wait_bytes(amp_z.at[step], zrecv_sem.at[0, step])
        wait_bytes(near.at[step, 0], nrecv_sem.at[0, step])
        wait_bytes(near.at[step, 1], nrecv_sem.at[1, step])

    def multiply(step, which):
        rows = GROUP * 16
        lhs = (amp_z[step] if which else own[step, :, 0:16, :]).reshape(rows, columns)
        for n in range(NX):
            at = slice(NY * n, NY * (n + 1))
            rhs = jnp.concatenate([
                own[step, at, 16:32, :].reshape(64, columns), int_z[step, at].reshape(64, columns),
                near[step, 0, at].reshape(64, columns), near[step, 1, at].reshape(64, columns),
            ], axis=0)
            term = lax.dot_general(lhs, rhs, (((1,), (1,)), ((), ())), preferred_element_type=jnp.float32)
            total[n, which] += term.reshape(NX, NY, 16, 256)

    state = pack(0, (jnp.int32(0), jnp.int32(0)))
    pl.semaphore_wait(barrier, len(everyone))
    send(0)
    for step in range(1, ahead):
        state = pack(step, state)
        send(step)

    def behind(step):
        @pl.when(step > 0)
        def _():
            relay(step - 1)

        @pl.when(step > 1)
        def _():
            arrive(step - 2)
            multiply(step - 2, 1)
            multiply(step - 2, 0)

    def turn(step, state):
        pass_on(step)
        state = pack(step + ahead, state)
        send(step + ahead)
        behind(step)
        return state

    lax.fori_loop(0, steps - ahead, turn, state)

    def late(step, carry):
        pass_on(step)
        behind(step)
        return carry

    lax.fori_loop(steps - ahead, steps, late, 0)
    relay(steps - 1)
    arrive(steps - 2)
    multiply(steps - 2, 1)
    multiply(steps - 2, 0)
    arrive(steps - 1)

    def scatter_first(which):
        for d in (1, 2, 3):
            px, py = lax.rem(x + d, NX), lax.rem(y + d, NY)
            pltpu.make_async_remote_copy(
                src_ref=total.at[0:2, which, px], dst_ref=part_x.at[which, d - 1],
                send_sem=rsend_sem.at[0, which], recv_sem=rrecv_sem.at[0, which],
                device_id=device(px, c, y, z), device_id_type=MESH,
            ).start()
            pltpu.make_async_remote_copy(
                src_ref=total.at[2:4, which, :, py], dst_ref=part_y.at[which, d - 1],
                send_sem=rsend_sem.at[1, which], recv_sem=rrecv_sem.at[1, which],
                device_id=device(x, c, py, z), device_id_type=MESH,
            ).start()

    def scatter_second(which):
        wait_bytes(part_x.at[which], rrecv_sem.at[0, which])
        sum_x[which] = total[0:2, which, x] + part_x[which, 0] + part_x[which, 1] + part_x[which, 2]
        for d in (1, 2, 3):
            py = lax.rem(y + d, NY)
            pltpu.make_async_remote_copy(
                src_ref=sum_x.at[which, :, py], dst_ref=end_y.at[which, d - 1],
                send_sem=rsend_sem.at[2, which], recv_sem=rrecv_sem.at[2, which],
                device_id=device(x, c, py, z), device_id_type=MESH,
            ).start()
        wait_bytes(part_y.at[which], rrecv_sem.at[1, which])
        sum_y[which] = total[2:4, which, :, y] + part_y[which, 0] + part_y[which, 1] + part_y[which, 2]
        for d in (1, 2, 3):
            px = lax.rem(x + d, NX)
            pltpu.make_async_remote_copy(
                src_ref=sum_y.at[which, :, px], dst_ref=end_x.at[which, d - 1],
                send_sem=rsend_sem.at[3, which], recv_sem=rrecv_sem.at[3, which],
                device_id=device(px, c, y, z), device_id_type=MESH,
            ).start()

    def finish(which):
        wait_bytes(end_y.at[which], rrecv_sem.at[2, which])
        done[which, 0:2] = sum_x[which, :, y] + end_y[which, 0] + end_y[which, 1] + end_y[which, 2]
        wait_bytes(end_x.at[which], rrecv_sem.at[3, which])
        done[which, 2:4] = sum_y[which, :, x] + end_x[which, 0] + end_x[which, 1] + end_x[which, 2]

    def place(values, n, swap, upper):
        for j in range(2):
            piece = values[:, j * BW:(j + 1) * BW]
            piece = jnp.where(swap == 1, pltpu.roll(piece, BW // 2, 1), piece)
            core = c if j == 0 else 1 - c
            start = pl.multiple_of((2 * n + core) * 2 * BW + upper * BW, BW)
            out_ref[:, pl.ds(start, BW)] = piece

    odd, high = lax.rem(z, 2), z // 2
    multiply(steps - 1, 1)
    scatter_first(1)
    multiply(steps - 1, 0)
    scatter_first(0)
    scatter_second(1)
    finish(1)
    copy = pltpu.make_async_remote_copy(
        src_ref=done.at[1], dst_ref=other, send_sem=last_sem.at[0], recv_sem=last_sem.at[1],
        device_id=amp_peer, device_id_type=MESH,
    )
    copy.start()
    scatter_second(0)
    copy.wait()
    for n in range(NX):
        place(other[n], n, 1 - odd, 1 - high)
    finish(0)
    for n in range(NX):
        place(done[0, n], n, odd, high)

    for which in range(2):
        wait_bytes(part_x.at[which], rsend_sem.at[0, which])
        wait_bytes(part_y.at[which], rsend_sem.at[1, which])
        wait_bytes(end_y.at[which], rsend_sem.at[2, which])
        wait_bytes(end_x.at[which], rsend_sem.at[3, which])
    wait_bytes(packed.at[:, 0:GROUP - 1], send_sem)
    wait_bytes(own, zsend_sem)
    wait_bytes(near, nsend_sem)


def solution(mesh):
    steps, ahead = 32, 4

    def shards(integrals, amplitudes, block_lists):
        columns = LISTED * BW // GROUP // steps
        f32, bf16 = jnp.float32, jnp.bfloat16
        return pl.pallas_call(
            functools.partial(kernel, steps, ahead),
            out_shape=jax.ShapeDtypeStruct((16, 2048), f32),
            in_specs=[
                pl.BlockSpec(memory_space=pltpu.SMEM),
                pl.BlockSpec(memory_space=pl.ANY),
                pl.BlockSpec(memory_space=pl.ANY),
            ],
            out_specs=pl.BlockSpec(memory_space=pltpu.VMEM),
            scratch_shapes=[
                pltpu.VMEM(amplitudes.shape, bf16),
                pltpu.VMEM(integrals.shape, bf16),
                pltpu.VMEM((steps, GROUP, 32, columns), bf16),
                pltpu.VMEM((steps, GROUP, 32, columns), bf16),
                pltpu.VMEM((steps, GROUP, 16, columns), bf16),
                pltpu.VMEM((steps, GROUP, 16, columns), bf16),
                pltpu.VMEM((steps, 2, GROUP, 16, columns), bf16),
                pltpu.VMEM((NX, 2, NX, NY, 16, 256), f32),
                pltpu.VMEM((2, 3, 2, NY, 16, 256), f32),
                pltpu.VMEM((2, 3, 2, NX, 16, 256), f32),
                pltpu.VMEM((2, 2, NY, 16, 256), f32),
                pltpu.VMEM((2, 2, NX, 16, 256), f32),
                pltpu.VMEM((2, 3, 2, 16, 256), f32),
                pltpu.VMEM((2, 3, 2, 16, 256), f32),
                pltpu.VMEM((2, NX, 16, 256), f32),
                pltpu.VMEM((NX, 16, 256), f32),
                pltpu.SemaphoreType.DMA((2,)),
                pltpu.SemaphoreType.DMA,
                pltpu.SemaphoreType.DMA((steps,)),
                pltpu.SemaphoreType.DMA,
                pltpu.SemaphoreType.DMA((2, steps)),
                pltpu.SemaphoreType.DMA,
                pltpu.SemaphoreType.DMA((2, steps)),
                pltpu.SemaphoreType.DMA((4, 2)),
                pltpu.SemaphoreType.DMA((4, 2)),
                pltpu.SemaphoreType.DMA((2,)),
            ],
            compiler_params=pltpu.CompilerParams(
                collective_id=0, has_side_effects=True, vmem_limit_bytes=62 * MIB
            ),
            name="ladder",
        )(block_lists.T, amplitudes, integrals)

    return jax.shard_map(
        shards,
        mesh=mesh,
        in_specs=(P(("vc", "vd"), None), P(("vc", "vd"), None), P()),
        out_specs=P(("vc", "vd"), None),
        check_vma=False,
    )
```

```python
import functools
import random

import jax
import jax.numpy as jnp
from jax import lax
from jax.experimental import pallas as pl
from jax.experimental.pallas import tpu as pltpu
from jax.sharding import PartitionSpec as P

MESH = pl.DeviceIdType.MESH
BW = 128
NX, NC, NY, NZ = 4, 2, 4, 4
GROUP = NX * NY
LISTED = 1024
MIB = 1 << 20


def device(x, c, y, z):
    return (x * NC + c, z * NY + y)


def wait_bytes(ref, sem):
    pltpu.make_async_copy(ref, ref, sem).wait()


def kernel(
    steps, ahead, lists, amp_hbm, int_hbm, out_ref,
    amp, integ, packed, own, amp_z, int_z, near, total, part_x, part_y, sum_x, sum_y, end_y, end_x, done,
    load_sem, send_sem, recv_sem, zsend_sem, zrecv_sem, nsend_sem, nrecv_sem, rsend_sem, rrecv_sem,
):
    vc, vd = lax.axis_index("vc"), lax.axis_index("vd")
    x, c, z, y = vc // NC, lax.rem(vc, NC), vd // NY, lax.rem(vd, NY)
    me = x * NY + y
    amp_peer = device(x, c, y, 3 - z)
    int_peer = device(x, c, y, z + 1 - 2 * lax.rem(z, 2))
    near_peer = device(x, 1 - c, y, z)
    order = [(dx, dy) for dx in range(NX) for dy in range(NY)][1:]
    random.Random(1).shuffle(order)
    peers = []
    for dx, dy in order:
        px, py = lax.rem(x + dx, NX), lax.rem(y + dy, NY)
        peers.append((px * NY + py, device(px, c, py, z)))
    columns = packed.shape[3]
    blocks = columns // BW
    slots, owners = lists.shape

    loads = [
        pltpu.make_async_copy(amp_hbm, amp, load_sem.at[0]),
        pltpu.make_async_copy(int_hbm, integ, load_sem.at[1]),
    ]
    for load in loads:
        load.start()
    barrier = pltpu.get_barrier_semaphore()
    across = [device(x, c, lax.rem(y + d, NY), 3 - z) for d in (1, 2, 3)]
    across += [device(lax.rem(x + d, NX), c, y, 3 - z) for d in (1, 2, 3)]
    everyone = [place for _, place in peers] + across + [amp_peer, int_peer, near_peer]
    for place in everyone:
        pl.semaphore_signal(barrier, inc=1, device_id=place, device_id_type=MESH)
    total[...] = jnp.zeros_like(total)
    for load in loads:
        load.wait()

    def pack(step, state):
        def one(member, state):
            owner, slot = state
            for block in range(blocks):
                start = lists[slot, owner] * BW
                packed[step, member, 0:16, block * BW:(block + 1) * BW] = amp[:, pl.ds(start, BW)]
                packed[step, member, 16:32, block * BW:(block + 1) * BW] = integ[:, pl.ds(start, BW)]
                following = lists[jnp.minimum(slot + 1, slots - 1), owner]
                stays = jnp.logical_and(slot + 1 < slots, following >= 0)
                slot = jnp.where(stays, slot + 1, 0)
                owner = jnp.minimum(jnp.where(stays, owner, owner + 1), owners - 1)
            return owner, slot

        return lax.fori_loop(0, GROUP, one, state)

    def send(step):
        for index, place in peers:
            pltpu.make_async_remote_copy(
                src_ref=packed.at[step, index], dst_ref=own.at[step, me],
                send_sem=send_sem, recv_sem=recv_sem.at[step], device_id=place, device_id_type=MESH,
            ).start()
        pltpu.make_async_copy(packed.at[step, me], own.at[step, me], recv_sem.at[step]).start()

    def pass_on(step):
        wait_bytes(own.at[step], recv_sem.at[step])
        pltpu.make_async_remote_copy(
            src_ref=own.at[step, :, 16:32, :], dst_ref=int_z.at[step],
            send_sem=zsend_sem, recv_sem=zrecv_sem.at[1, step], device_id=int_peer, device_id_type=MESH,
        ).start()
        pltpu.make_async_remote_copy(
            src_ref=own.at[step, :, 0:16, :], dst_ref=amp_z.at[step],
            send_sem=zsend_sem, recv_sem=zrecv_sem.at[0, step], device_id=amp_peer, device_id_type=MESH,
        ).start()
        pltpu.make_async_remote_copy(
            src_ref=own.at[step, :, 16:32, :], dst_ref=near.at[step, 0],
            send_sem=nsend_sem, recv_sem=nrecv_sem.at[0, step], device_id=near_peer, device_id_type=MESH,
        ).start()

    def relay(step):
        wait_bytes(int_z.at[step], zrecv_sem.at[1, step])
        pltpu.make_async_remote_copy(
            src_ref=int_z.at[step], dst_ref=near.at[step, 1],
            send_sem=nsend_sem, recv_sem=nrecv_sem.at[1, step], device_id=near_peer, device_id_type=MESH,
        ).start()

    def multiply(step, row, col):
        rows = GROUP * 16
        lhs = (amp_z[step] if row else own[step, :, 0:16, :]).reshape(rows, columns)
        for pair in range(NX // 2):
            pieces = []
            for n in (2 * pair, 2 * pair + 1):
                at = slice(NY * n, NY * (n + 1))
                pieces.append((int_z[step, at] if col else own[step, at, 16:32, :]).reshape(64, columns))
                pieces.append(near[step, col, at].reshape(64, columns))
            rhs = jnp.concatenate(pieces, axis=0)
            term = lax.dot_general(lhs, rhs, (((1,), (1,)), ((), ())), preferred_element_type=jnp.float32)
            for i in range(2):
                part = term[:, i * BW:(i + 1) * BW].reshape(NX, NY, 16, BW)
                if pair == 0:
                    total[row, col, 0, :, i] += part
                else:
                    for k in range(NX):
                        total[row, col, 1, :, i, k] += part[k]

    def arrive_rows(step):
        wait_bytes(amp_z.at[step], zrecv_sem.at[0, step])

    def arrive_near(step, col):
        wait_bytes(near.at[step, col], nrecv_sem.at[col, step])

    state = pack(0, (jnp.int32(0), jnp.int32(0)))
    pl.semaphore_wait(barrier, len(everyone))
    send(0)
    for step in range(1, ahead):
        state = pack(step, state)
        send(step)

    def behind(step):
        @pl.when(step > 0)
        def _():
            relay(step - 1)

        @pl.when(step > 1)
        def _():
            arrive_near(step - 2, 0)
            arrive_rows(step - 2)
            arrive_near(step - 2, 1)
            for row in range(2):
                for col in range(2):
                    multiply(step - 2, row, col)

    def turn(step, state):
        pass_on(step)
        state = pack(step + ahead, state)
        send(step + ahead)
        behind(step)
        return state

    lax.fori_loop(0, steps - ahead, turn, state)

    def late(step, carry):
        pass_on(step)
        behind(step)
        return carry

    lax.fori_loop(steps - ahead, steps, late, 0)

    def scatter_first(row, col):
        q = 2 * row + col
        for d in (1, 2, 3):
            px, py = lax.rem(x + d, NX), lax.rem(y + d, NY)
            pltpu.make_async_remote_copy(
                src_ref=total.at[row, col, 0, px], dst_ref=part_x.at[q, d - 1],
                send_sem=rsend_sem.at[0, q], recv_sem=rrecv_sem.at[0, q],
                device_id=device(px, c, y, z), device_id_type=MESH,
            ).start()
            pltpu.make_async_remote_copy(
                src_ref=total.at[row, col, 1, py], dst_ref=part_y.at[q, d - 1],
                send_sem=rsend_sem.at[1, q], recv_sem=rrecv_sem.at[1, q],
                device_id=device(x, c, py, z), device_id_type=MESH,
            ).start()

    def scatter_second(row, col):
        q = 2 * row + col
        wait_bytes(part_x.at[q], rrecv_sem.at[0, q])
        for i in range(2):
            sum_x[q, :, i] = total[row, col, 0, x, i] + part_x[q, 0, i] + part_x[q, 1, i] + part_x[q, 2, i]
        for d in range(1 - row, 4):
            py = lax.rem(y + d, NY)
            pltpu.make_async_remote_copy(
                src_ref=sum_x.at[q, py], dst_ref=end_y.at[q, d],
                send_sem=rsend_sem.at[2, q], recv_sem=rrecv_sem.at[2, q],
                device_id=device(x, c, py, 3 - z if row else z), device_id_type=MESH,
            ).start()
        wait_bytes(part_y.at[q], rrecv_sem.at[1, q])
        for i in range(2):
            sum_y[q, :, i] = total[row, col, 1, y, i] + part_y[q, 0, i] + part_y[q, 1, i] + part_y[q, 2, i]
        for d in range(1 - row, 4):
            px = lax.rem(x + d, NX)
            pltpu.make_async_remote_copy(
                src_ref=sum_y.at[q, px], dst_ref=end_x.at[q, d],
                send_sem=rsend_sem.at[3, q], recv_sem=rrecv_sem.at[3, q],
                device_id=device(px, c, y, 3 - z if row else z), device_id_type=MESH,
            ).start()

    def finish(row, col):
        q = 2 * row + col
        wait_bytes(end_y.at[q, 1 - row:4], rrecv_sem.at[2, q])
        mine = end_y[q, 0] if row else sum_x[q, y]
        done[q, 0:2] = mine + end_y[q, 1] + end_y[q, 2] + end_y[q, 3]
        wait_bytes(end_x.at[q, 1 - row:4], rrecv_sem.at[3, q])
        mine = end_x[q, 0] if row else sum_y[q, x]
        done[q, 2:4] = mine + end_x[q, 1] + end_x[q, 2] + end_x[q, 3]

    def place(own_part, partner_part, odd, upper):
        lower_lanes = lax.broadcasted_iota(jnp.int32, (16, BW), 1) < BW // 2
        for n in range(NX):
            first = jnp.where(odd == 1, partner_part[n], own_part[n])
            second = jnp.where(odd == 1, own_part[n], partner_part[n])
            pieces = (
                jnp.where(lower_lanes, first, pltpu.roll(second, BW // 2, 1)),
                jnp.where(lower_lanes, pltpu.roll(first, BW // 2, 1), second),
            )
            for core, piece in zip((c, 1 - c), pieces):
                start = pl.multiple_of((2 * n + core) * 2 * BW + upper * BW, BW)
                out_ref[:, pl.ds(start, BW)] = piece

    for step in (steps - 2, steps - 1):
        arrive_near(step, 0)
        multiply(step, 0, 0)
    scatter_first(0, 0)
    relay(steps - 1)
    arrive_rows(steps - 2)
    multiply(steps - 2, 1, 0)
    arrive_near(steps - 2, 1)
    multiply(steps - 2, 1, 1)
    multiply(steps - 2, 0, 1)
    arrive_rows(steps - 1)
    multiply(steps - 1, 1, 0)
    scatter_first(1, 0)
    scatter_second(0, 0)
    arrive_near(steps - 1, 1)
    multiply(steps - 1, 1, 1)
    scatter_first(1, 1)
    multiply(steps - 1, 0, 1)
    scatter_second(1, 0)
    scatter_first(0, 1)
    finish(0, 0)
    scatter_second(1, 1)
    finish(1, 0)
    scatter_second(0, 1)
    finish(1, 1)
    finish(0, 1)
    odd, high = lax.rem(z, 2), z // 2
    place(done.at[0], done.at[1], odd, high)
    place(done.at[2], done.at[3], 1 - odd, 1 - high)

    for q in range(4):
        wait_bytes(part_x.at[q], rsend_sem.at[0, q])
        wait_bytes(part_y.at[q], rsend_sem.at[1, q])
        wait_bytes(end_y.at[q, 1 - q // 2:4], rsend_sem.at[2, q])
        wait_bytes(end_x.at[q, 1 - q // 2:4], rsend_sem.at[3, q])
    wait_bytes(packed.at[:, 0:GROUP - 1], send_sem)
    wait_bytes(own, zsend_sem)
    wait_bytes(near, nsend_sem)


def solution(mesh):
    steps, ahead = 32, 4

    def shards(integrals, amplitudes, block_lists):
        columns = LISTED * BW // GROUP // steps
        f32, bf16 = jnp.float32, jnp.bfloat16
        return pl.pallas_call(
            functools.partial(kernel, steps, ahead),
            out_shape=jax.ShapeDtypeStruct((16, 2048), f32),
            in_specs=[
                pl.BlockSpec(memory_space=pltpu.SMEM),
                pl.BlockSpec(memory_space=pl.ANY),
                pl.BlockSpec(memory_space=pl.ANY),
            ],
            out_specs=pl.BlockSpec(memory_space=pltpu.VMEM),
            scratch_shapes=[
                pltpu.VMEM(amplitudes.shape, bf16),
                pltpu.VMEM(integrals.shape, bf16),
                pltpu.VMEM((steps, GROUP, 32, columns), bf16),
                pltpu.VMEM((steps, GROUP, 32, columns), bf16),
                pltpu.VMEM((steps, GROUP, 16, columns), bf16),
                pltpu.VMEM((steps, GROUP, 16, columns), bf16),
                pltpu.VMEM((steps, 2, GROUP, 16, columns), bf16),
                pltpu.VMEM((2, 2, 2, NX, 2, NY, 16, BW), f32),
                pltpu.VMEM((4, 3, 2, NY, 16, BW), f32),
                pltpu.VMEM((4, 3, 2, NX, 16, BW), f32),
                pltpu.VMEM((4, NY, 2, 16, BW), f32),
                pltpu.VMEM((4, NX, 2, 16, BW), f32),
                pltpu.VMEM((4, 4, 2, 16, BW), f32),
                pltpu.VMEM((4, 4, 2, 16, BW), f32),
                pltpu.VMEM((4, NX, 16, BW), f32),
                pltpu.SemaphoreType.DMA((2,)),
                pltpu.SemaphoreType.DMA,
                pltpu.SemaphoreType.DMA((steps,)),
                pltpu.SemaphoreType.DMA,
                pltpu.SemaphoreType.DMA((2, steps)),
                pltpu.SemaphoreType.DMA,
                pltpu.SemaphoreType.DMA((2, steps)),
                pltpu.SemaphoreType.DMA((4, 4)),
                pltpu.SemaphoreType.DMA((4, 4)),
            ],
            compiler_params=pltpu.CompilerParams(
                collective_id=0, has_side_effects=True, vmem_limit_bytes=62 * MIB
            ),
            name="ladder",
        )(block_lists.T, amplitudes, integrals)

    return jax.shard_map(
        shards,
        mesh=mesh,
        in_specs=(P(("vc", "vd"), None), P(("vc", "vd"), None), P()),
        out_specs=P(("vc", "vd"), None),
        check_vma=False,
    )
```

```python
import functools
import random

import jax
import jax.numpy as jnp
from jax import lax
from jax.experimental import pallas as pl
from jax.experimental.pallas import tpu as pltpu
from jax.sharding import PartitionSpec as P

MESH = pl.DeviceIdType.MESH
BW = 128
NX, NC, NY, NZ = 4, 2, 4, 4
GROUP = NX * NY
LISTED = 1024
MIB = 1 << 20


def device(x, c, y, z):
    return (x * NC + c, z * NY + y)


def wait_bytes(ref, sem):
    pltpu.make_async_copy(ref, ref, sem).wait()


def kernel(
    steps, ahead, relay_lag, lag, lists, amp_hbm, int_hbm, out_ref,
    amp, integ, packed, own, amp_z, int_z, near, total, part_x, part_y, sum_x, sum_y, end_y, end_x, done,
    load_sem, send_sem, recv_sem, zsend_sem, zrecv_sem, nsend_sem, nrecv_sem, rsend_sem, rrecv_sem,
):
    vc, vd = lax.axis_index("vc"), lax.axis_index("vd")
    x, c, z, y = vc // NC, lax.rem(vc, NC), vd // NY, lax.rem(vd, NY)
    me = x * NY + y
    amp_peer = device(x, c, y, 3 - z)
    int_peer = device(x, c, y, z + 1 - 2 * lax.rem(z, 2))
    near_peer = device(x, 1 - c, y, z)
    order = [(dx, dy) for dx in range(NX) for dy in range(NY)][1:]
    random.Random(1).shuffle(order)
    peers = []
    for dx, dy in order:
        px, py = lax.rem(x + dx, NX), lax.rem(y + dy, NY)
        peers.append((px * NY + py, device(px, c, py, z)))
    columns = packed.shape[3]
    blocks = columns // BW
    slots, owners = lists.shape

    loads = [
        pltpu.make_async_copy(amp_hbm, amp, load_sem.at[0]),
        pltpu.make_async_copy(int_hbm, integ, load_sem.at[1]),
    ]
    for load in loads:
        load.start()
    barrier = pltpu.get_barrier_semaphore()
    across = [device(x, c, lax.rem(y + d, NY), 3 - z) for d in (1, 2, 3)]
    across += [device(lax.rem(x + d, NX), c, y, 3 - z) for d in (1, 2, 3)]
    everyone = [place for _, place in peers] + across + [amp_peer, int_peer, near_peer]
    for place in everyone:
        pl.semaphore_signal(barrier, inc=1, device_id=place, device_id_type=MESH)
    total[...] = jnp.zeros_like(total)
    for load in loads:
        load.wait()

    def pack(step, state):
        def one(member, state):
            owner, slot = state
            for block in range(blocks):
                start = lists[slot, owner] * BW
                packed[step, member, 0:16, block * BW:(block + 1) * BW] = amp[:, pl.ds(start, BW)]
                packed[step, member, 16:32, block * BW:(block + 1) * BW] = integ[:, pl.ds(start, BW)]
                following = lists[jnp.minimum(slot + 1, slots - 1), owner]
                stays = jnp.logical_and(slot + 1 < slots, following >= 0)
                slot = jnp.where(stays, slot + 1, 0)
                owner = jnp.minimum(jnp.where(stays, owner, owner + 1), owners - 1)
            return owner, slot

        return lax.fori_loop(0, GROUP, one, state)

    def send(step):
        for index, place in peers:
            pltpu.make_async_remote_copy(
                src_ref=packed.at[step, index], dst_ref=own.at[step, me],
                send_sem=send_sem, recv_sem=recv_sem.at[step], device_id=place, device_id_type=MESH,
            ).start()
        pltpu.make_async_copy(packed.at[step, me], own.at[step, me], recv_sem.at[step]).start()

    def pass_on(step):
        wait_bytes(own.at[step], recv_sem.at[step])
        pltpu.make_async_remote_copy(
            src_ref=own.at[step, :, 16:32, :], dst_ref=int_z.at[step],
            send_sem=zsend_sem, recv_sem=zrecv_sem.at[1, step], device_id=int_peer, device_id_type=MESH,
        ).start()
        pltpu.make_async_remote_copy(
            src_ref=own.at[step, :, 0:16, :], dst_ref=amp_z.at[step],
            send_sem=zsend_sem, recv_sem=zrecv_sem.at[0, step], device_id=amp_peer, device_id_type=MESH,
        ).start()
        pltpu.make_async_remote_copy(
            src_ref=own.at[step, :, 16:32, :], dst_ref=near.at[step, 0],
            send_sem=nsend_sem, recv_sem=nrecv_sem.at[0, step], device_id=near_peer, device_id_type=MESH,
        ).start()

    def relay(step):
        wait_bytes(int_z.at[step], zrecv_sem.at[1, step])
        pltpu.make_async_remote_copy(
            src_ref=int_z.at[step], dst_ref=near.at[step, 1],
            send_sem=nsend_sem, recv_sem=nrecv_sem.at[1, step], device_id=near_peer, device_id_type=MESH,
        ).start()

    def multiply(step, row, col):
        rows = GROUP * 16
        lhs = (amp_z[step] if row else own[step, :, 0:16, :]).reshape(rows, columns)
        for pair in range(NX // 2):
            pieces = []
            for n in (2 * pair, 2 * pair + 1):
                at = slice(NY * n, NY * (n + 1))
                pieces.append((int_z[step, at] if col else own[step, at, 16:32, :]).reshape(64, columns))
                pieces.append(near[step, col, at].reshape(64, columns))
            rhs = jnp.concatenate(pieces, axis=0)
            term = lax.dot_general(lhs, rhs, (((1,), (1,)), ((), ())), preferred_element_type=jnp.float32)
            for i in range(2):
                part = term[:, i * BW:(i + 1) * BW].reshape(NX, NY, 16, BW)
                if pair == 0:
                    total[row, col, 0, :, i] += part
                else:
                    for k in range(NX):
                        total[row, col, 1, :, i, k] += part[k]

    def arrive_rows(step):
        wait_bytes(amp_z.at[step], zrecv_sem.at[0, step])

    def arrive_near(step, col):
        wait_bytes(near.at[step, col], nrecv_sem.at[col, step])

    state = pack(0, (jnp.int32(0), jnp.int32(0)))
    pl.semaphore_wait(barrier, len(everyone))
    send(0)
    for step in range(1, ahead):
        state = pack(step, state)
        send(step)

    def settle(step):
        arrive_rows(step)
        arrive_near(step, 1)
        multiply(step, 1, 0)
        multiply(step, 1, 1)
        multiply(step, 0, 1)

    def behind(step):
        @pl.when(step >= relay_lag)
        def _():
            relay(step - relay_lag)

        @pl.when(step >= lag)
        def _():
            arrive_near(step - lag, 0)
            arrive_rows(step - lag)
            arrive_near(step - lag, 1)
            for row in range(2):
                for col in range(2):
                    multiply(step - lag, row, col)

    def turn(step, state):
        pass_on(step)
        state = pack(step + ahead, state)
        send(step + ahead)
        behind(step)
        return state

    lax.fori_loop(0, steps - ahead, turn, state)

    def late(step, carry):
        pass_on(step)
        behind(step)
        return carry

    lax.fori_loop(steps - ahead, steps, late, 0)

    def scatter_first(row, col):
        q = 2 * row + col
        for d in (2, 1, 3):
            px, py = lax.rem(x + d, NX), lax.rem(y + d, NY)
            pltpu.make_async_remote_copy(
                src_ref=total.at[row, col, 0, px], dst_ref=part_x.at[q, d - 1],
                send_sem=rsend_sem.at[0, q], recv_sem=rrecv_sem.at[0, q],
                device_id=device(px, c, y, z), device_id_type=MESH,
            ).start()
            pltpu.make_async_remote_copy(
                src_ref=total.at[row, col, 1, py], dst_ref=part_y.at[q, d - 1],
                send_sem=rsend_sem.at[1, q], recv_sem=rrecv_sem.at[1, q],
                device_id=device(x, c, py, z), device_id_type=MESH,
            ).start()

    def scatter_second(row, col):
        q = 2 * row + col
        wait_bytes(part_x.at[q], rrecv_sem.at[0, q])
        for i in range(2):
            sum_x[q, :, i] = total[row, col, 0, x, i] + part_x[q, 0, i] + part_x[q, 1, i] + part_x[q, 2, i]
        for d in range(1 - row, 4):
            py = lax.rem(y + d, NY)
            pltpu.make_async_remote_copy(
                src_ref=sum_x.at[q, py], dst_ref=end_y.at[q, d],
                send_sem=rsend_sem.at[2, q], recv_sem=rrecv_sem.at[2, q],
                device_id=device(x, c, py, 3 - z if row else z), device_id_type=MESH,
            ).start()
        wait_bytes(part_y.at[q], rrecv_sem.at[1, q])
        for i in range(2):
            sum_y[q, :, i] = total[row, col, 1, y, i] + part_y[q, 0, i] + part_y[q, 1, i] + part_y[q, 2, i]
        for d in range(1 - row, 4):
            px = lax.rem(x + d, NX)
            pltpu.make_async_remote_copy(
                src_ref=sum_y.at[q, px], dst_ref=end_x.at[q, d],
                send_sem=rsend_sem.at[3, q], recv_sem=rrecv_sem.at[3, q],
                device_id=device(px, c, y, 3 - z if row else z), device_id_type=MESH,
            ).start()

    def finish(row, col):
        q = 2 * row + col
        wait_bytes(end_y.at[q, 1 - row:4], rrecv_sem.at[2, q])
        mine = end_y[q, 0] if row else sum_x[q, y]
        done[q, 0:2] = mine + end_y[q, 1] + end_y[q, 2] + end_y[q, 3]
        wait_bytes(end_x.at[q, 1 - row:4], rrecv_sem.at[3, q])
        mine = end_x[q, 0] if row else sum_y[q, x]
        done[q, 2:4] = mine + end_x[q, 1] + end_x[q, 2] + end_x[q, 3]

    def place(own_part, partner_part, odd, upper):
        lower_lanes = lax.broadcasted_iota(jnp.int32, (16, BW), 1) < BW // 2
        for n in range(NX):
            first = jnp.where(odd == 1, partner_part[n], own_part[n])
            second = jnp.where(odd == 1, own_part[n], partner_part[n])
            pieces = (
                jnp.where(lower_lanes, first, pltpu.roll(second, BW // 2, 1)),
                jnp.where(lower_lanes, pltpu.roll(first, BW // 2, 1), second),
            )
            for core, piece in zip((c, 1 - c), pieces):
                start = pl.multiple_of((2 * n + core) * 2 * BW + upper * BW, BW)
                out_ref[:, pl.ds(start, BW)] = piece

    for step in range(steps - relay_lag, steps - 2):
        relay(step)
    for step in range(steps - lag, steps):
        arrive_near(step, 0)
        multiply(step, 0, 0)
    scatter_first(0, 0)
    if relay_lag > 1:
        relay(steps - 2)
    for step in range(steps - lag, steps - 1):
        settle(step)
    relay(steps - 1)
    arrive_rows(steps - 1)
    multiply(steps - 1, 1, 0)
    scatter_first(1, 0)
    scatter_second(0, 0)
    arrive_near(steps - 1, 1)
    multiply(steps - 1, 1, 1)
    scatter_first(1, 1)
    multiply(steps - 1, 0, 1)
    scatter_second(1, 0)
    scatter_first(0, 1)
    finish(0, 0)
    scatter_second(1, 1)
    scatter_second(0, 1)
    odd, high = lax.rem(z, 2), z // 2
    finish(1, 0)
    finish(1, 1)
    place(done.at[2], done.at[3], 1 - odd, 1 - high)
    finish(0, 1)
    place(done.at[0], done.at[1], odd, high)

    for q in range(4):
        wait_bytes(part_x.at[q], rsend_sem.at[0, q])
        wait_bytes(part_y.at[q], rsend_sem.at[1, q])
        wait_bytes(end_y.at[q, 1 - q // 2:4], rsend_sem.at[2, q])
        wait_bytes(end_x.at[q, 1 - q // 2:4], rsend_sem.at[3, q])
    wait_bytes(packed.at[:, 0:GROUP - 1], send_sem)
    wait_bytes(own, zsend_sem)
    wait_bytes(near, nsend_sem)


def solution(mesh):
    steps, ahead, relay_lag, lag = 32, 6, 2, 4

    def shards(integrals, amplitudes, block_lists):
        columns = LISTED * BW // GROUP // steps
        f32, bf16 = jnp.float32, jnp.bfloat16
        return pl.pallas_call(
            functools.partial(kernel, steps, ahead, relay_lag, lag),
            out_shape=jax.ShapeDtypeStruct((16, 2048), f32),
            in_specs=[
                pl.BlockSpec(memory_space=pltpu.SMEM),
                pl.BlockSpec(memory_space=pl.ANY),
                pl.BlockSpec(memory_space=pl.ANY),
            ],
            out_specs=pl.BlockSpec(memory_space=pltpu.VMEM),
            scratch_shapes=[
                pltpu.VMEM(amplitudes.shape, bf16),
                pltpu.VMEM(integrals.shape, bf16),
                pltpu.VMEM((steps, GROUP, 32, columns), bf16),
                pltpu.VMEM((steps, GROUP, 32, columns), bf16),
                pltpu.VMEM((steps, GROUP, 16, columns), bf16),
                pltpu.VMEM((steps, GROUP, 16, columns), bf16),
                pltpu.VMEM((steps, 2, GROUP, 16, columns), bf16),
                pltpu.VMEM((2, 2, 2, NX, 2, NY, 16, BW), f32),
                pltpu.VMEM((4, 3, 2, NY, 16, BW), f32),
                pltpu.VMEM((4, 3, 2, NX, 16, BW), f32),
                pltpu.VMEM((4, NY, 2, 16, BW), f32),
                pltpu.VMEM((4, NX, 2, 16, BW), f32),
                pltpu.VMEM((4, 4, 2, 16, BW), f32),
                pltpu.VMEM((4, 4, 2, 16, BW), f32),
                pltpu.VMEM((4, NX, 16, BW), f32),
                pltpu.SemaphoreType.DMA((2,)),
                pltpu.SemaphoreType.DMA,
                pltpu.SemaphoreType.DMA((steps,)),
                pltpu.SemaphoreType.DMA,
                pltpu.SemaphoreType.DMA((2, steps)),
                pltpu.SemaphoreType.DMA,
                pltpu.SemaphoreType.DMA((2, steps)),
                pltpu.SemaphoreType.DMA((4, 4)),
                pltpu.SemaphoreType.DMA((4, 4)),
            ],
            compiler_params=pltpu.CompilerParams(
                collective_id=0, has_side_effects=True, vmem_limit_bytes=62 * MIB
            ),
            name="ladder",
        )(block_lists.T, amplitudes, integrals)

    return jax.shard_map(
        shards,
        mesh=mesh,
        in_specs=(P(("vc", "vd"), None), P(("vc", "vd"), None), P()),
        out_specs=P(("vc", "vd"), None),
        check_vma=False,
    )
```
